32 devices in a mesh: row: 8 (over y, x, core), col: 4 (over z).
Axes of the slice: x: 2, y: 2, z: 4, core: 2. Of those that a mesh axis runs over, the one named last changes fastest.
Arguments:
- layer_input: bfloat16 [384, 8192], P('col', 'row'), may hold values from -6 to 6
- out_grad: bfloat16 [384, 8192], P('col', 'row'), may hold values from -6 to 6
- gate_weight: bfloat16 [8192, 28672], P('row', 'col'), may hold values from -0.0625 to 0.0625
- up_weight: bfloat16 [8192, 28672], P('row', 'col'), may hold values from -0.0625 to 0.0625
- down_weight: bfloat16 [28672, 8192], P('col', 'row'), may hold values from -0.03125 to 0.03125
Outputs:
- input_grad: bfloat16 [384, 8192], P('col', 'row')
- gate_grad: bfloat16 [8192, 28672], P('row', 'col')
- up_grad: bfloat16 [8192, 28672], P('row', 'col')
- down_grad: bfloat16 [28672, 8192], P('col', 'row')
The draws below stay inside these ranges and needn't reach their ends.
All inputs are finite; a program needn't handle non-finite values.
Results may differ from the reference program's by a relative error of at most 0.033.
Values may be sent and summed in bfloat16 or wider, within the bound.
No kernel may reach another device: no remote copies, remote signals or barrier semaphores. Data moves between devices by JAX's collectives and lax.ppermute only.
A program may use at most 192 MiB of HBM per device.

```python
import jax
import jax.numpy as jnp
from jax import lax

D = 8192
FF = 28672
TOKENS = 384
N_ROW = 8


def levels(key, dims, pieces, smallest, top_value):
    level = 1.0
    for dim, blocks in pieces:
        draws = jax.random.uniform(jax.random.fold_in(jax.random.fold_in(key, 6), dim), (blocks,), jnp.float32, smallest / len(pieces), top_value / len(pieces))
        level = level * jnp.repeat(jnp.exp(draws), dims[dim] // blocks).reshape((-1,) + (1,) * (len(dims) - 1 - dim))
    return level


def scatter_about(key, shape, scale, reach, shards=(), kind=jnp.bfloat16):
    gain = levels(key, shape, shards, -0.22, 0.18) if shards else 1.0
    entries = jax.random.normal(key, shape, jnp.float32) * scale * gain
    return jnp.minimum(jnp.maximum(entries, -reach), reach).astype(kind)


def setup_inputs(seed: int = 0) -> dict:
    seeds = jax.random.split(jax.random.key(seed), 6)
    return {
        "layer_input": scatter_about(seeds[0], (TOKENS, D), 1.0, 6.0, ((0, 4), (1, 8))),
        "out_grad": scatter_about(seeds[1], (TOKENS, D), 1.0, 6.0, ((0, 4), (1, 8))),
        "gate_weight": scatter_about(seeds[2], (D, FF), D ** -0.5, 0.0625, ((0, 8), (1, 4))),
        "up_weight": scatter_about(seeds[3], (D, FF), D ** -0.5, 0.0625, ((0, 8), (1, 4))),
        "down_weight": scatter_about(seeds[4], (FF, D), FF ** -0.5, 0.03125, ((0, 4), (1, 8))),
    }


def block_sum(left, right, blocks):
    count = left.shape[0]
    width = left.shape[1] // blocks
    left_blocks = left.reshape(count, blocks, width).transpose(1, 0, 2)
    right_blocks = right.reshape(blocks, width, right.shape[1])

    def accumulate(total, pair):
        term = jnp.dot(pair[0], pair[1], preferred_element_type=jnp.float32).astype(jnp.bfloat16)
        term = lax.optimization_barrier(term)
        return total + term.astype(jnp.float32), None

    start = jnp.zeros((count, right.shape[1]), jnp.float32)
    total, unused = lax.scan(accumulate, start, (left_blocks, right_blocks))
    return total


def reference(layer_input, out_grad, gate_weight, up_weight, down_weight):
    gate = block_sum(layer_input, gate_weight, N_ROW)
    up = block_sum(layer_input, up_weight, N_ROW)
    hidden_grad = block_sum(out_grad, down_weight.T, N_ROW)
    sigma = jax.nn.sigmoid(gate)
    swish = gate * sigma
    hidden = (swish * up).astype(jnp.bfloat16)
    up_delta = (hidden_grad * swish).astype(jnp.bfloat16)
    gate_delta = (hidden_grad * up * sigma * (1.0 + gate * (1.0 - sigma))).astype(jnp.bfloat16)
    factor = 1.0 / (TOKENS ** 0.5)
    down_grad = (jnp.dot(hidden.T, out_grad, preferred_element_type=jnp.float32) * factor).astype(jnp.bfloat16)
    gate_grad = (jnp.dot(layer_input.T, gate_delta, preferred_element_type=jnp.float32) * factor).astype(jnp.bfloat16)
    up_grad = (jnp.dot(layer_input.T, up_delta, preferred_element_type=jnp.float32) * factor).astype(jnp.bfloat16)
    input_grad = jnp.dot(gate_delta, gate_weight.T, preferred_element_type=jnp.float32)
    input_grad = input_grad + jnp.dot(up_delta, up_weight.T, preferred_element_type=jnp.float32)
    return input_grad.astype(jnp.bfloat16), gate_grad, up_grad, down_grad
```

```python
import functools
import math

import jax
import jax.numpy as jnp
from jax import lax
from jax.experimental import pallas as pl
from jax.experimental.pallas import tpu as pltpu
from jax.sharding import PartitionSpec as P

BF16 = jnp.bfloat16
F32 = jnp.float32
LANES = 128
CONTRACT_LAST = (((1,), (1,)), ((), ()))
CONTRACT_FIRST = (((0,), (0,)), ((), ()))


def swiglu_back(gate, up, hidden_grad):
    sigma = jax.nn.sigmoid(gate)
    swish = gate * sigma
    hidden = (swish * up).astype(BF16)
    up_delta = (hidden_grad * swish).astype(BF16)
    gate_delta = (hidden_grad * up * sigma * (1.0 + gate * (1.0 - sigma))).astype(BF16)
    return (hidden, gate_delta, up_delta)


def plain(layer_input, out_grad, gate_weight, up_weight, down_weight):
    inputs, cots = (
        lax.all_gather(layer_input, "col", axis=0, tiled=True),
        lax.all_gather(out_grad, "col", axis=0, tiled=True),
    )
    tokens = inputs.shape[0]
    width = gate_weight.shape[1]
    both_weights = jnp.concatenate([gate_weight, up_weight], axis=1)
    gate_up = jnp.dot(inputs, both_weights, preferred_element_type=F32)
    hidden_grad = lax.dot_general(cots, down_weight, CONTRACT_LAST, preferred_element_type=F32)
    summed = lax.psum_scatter(
        jnp.concatenate([gate_up, hidden_grad], axis=1).astype(BF16),
        "row",
        scatter_dimension=0,
        tiled=True,
    ).astype(F32)
    hidden, gate_delta, up_delta = swiglu_back(
        summed[:, :width], summed[:, width : 2 * width], summed[:, 2 * width :]
    )
    hidden = lax.all_gather(hidden, "row", axis=0, tiled=True)
    gate_delta = lax.all_gather(gate_delta, "row", axis=0, tiled=True)
    up_delta = lax.all_gather(up_delta, "row", axis=0, tiled=True)
    down_sum = lax.dot_general(hidden, cots, CONTRACT_FIRST, preferred_element_type=F32)
    gate_sum = lax.dot_general(inputs, gate_delta, CONTRACT_FIRST, preferred_element_type=F32)
    up_sum = lax.dot_general(inputs, up_delta, CONTRACT_FIRST, preferred_element_type=F32)
    term = lax.dot_general(gate_delta, gate_weight, CONTRACT_LAST, preferred_element_type=F32)
    term = term + lax.dot_general(up_delta, up_weight, CONTRACT_LAST, preferred_element_type=F32)
    factor = 1.0 / tokens**0.5
    input_grad = lax.psum_scatter(term.astype(BF16), "col", scatter_dimension=0, tiled=True)
    return (
        input_grad,
        (gate_sum * factor).astype(BF16),
        (up_sum * factor).astype(BF16),
        (down_sum * factor).astype(BF16),
    )


class Chain:
    def __init__(self, token):
        self.token = token

    def call(self, kernel, name, table, ins, in_specs, outs, out_specs, scratch=(), aliases=None, after=(), spare=6):
        extra = [self.token, *after]
        n_in, n_extra, n_out = len(ins), len(extra), len(outs)

        def body(table_ref, *refs):
            in_refs = refs[:n_in]
            out_refs = refs[n_in + n_extra : n_in + n_extra + n_out]
            token_ref = refs[n_in + n_extra + n_out]
            scratch_refs = refs[n_in + n_extra + n_out + 1 :]
            token_ref[...] = jnp.zeros_like(token_ref)
            kernel(table_ref, in_refs, out_refs, scratch_refs)

        held = 0
        for kind in scratch:
            if kind.dtype in (BF16, F32):
                held += math.prod(kind.shape) * jnp.dtype(kind.dtype).itemsize
        *results, self.token = pl.pallas_call(
            body,
            name=name,
            grid_spec=pltpu.PrefetchScalarGridSpec(
                num_scalar_prefetch=1,
                grid=(),
                in_specs=[*in_specs, *[ANY] * n_extra],
                out_specs=[*out_specs, VMEM],
                scratch_shapes=list(scratch),
            ),
            out_shape=[*outs, jax.ShapeDtypeStruct((8, LANES), F32)],
            input_output_aliases={1 + i: o for i, o in (aliases or {}).items()},
            compiler_params=pltpu.CompilerParams(vmem_limit_bytes=held + spare * 2**20),
            cost_estimate=pl.CostEstimate(flops=COST, bytes_accessed=COST, transcendentals=0),
        )(table, *ins, *extra)
        return results


ANY = pl.BlockSpec(memory_space=pl.ANY)
VMEM = pl.BlockSpec(memory_space=pltpu.VMEM)
COST = 10**12
AHEAD = 3


def shape(dims, kind=BF16):
    return jax.ShapeDtypeStruct(dims, kind)


KEEP, SEND, NEAR, FAR = (0, 1, 2, 3), (4, 5, 6, 7), (8, 9, 10, 11), (12, 13, 14, 15)


def place(table_ref, entry, start, w):
    return pl.ds(pl.multiple_of(start + table_ref[entry] * w, LANES), w)


def gather_tokens(chain, table, parts, after=()):
    two, own_rows, depth = parts[0].shape
    count = len(parts)

    def kernel(table_ref, ins, outs, _):
        for i in range(count):
            outs[0][:, i * own_rows : (i + 1) * own_rows] = ins[i][...]

    (out,) = chain.call(
        kernel, "gather_tokens", table, parts, [VMEM] * count, [shape((two, count * own_rows, depth))], [VMEM],
        after=after, spare=4,
    )
    return out


def down_copy_of(columns, down_ref, held, sems, slot):
    return pltpu.make_async_copy(down_ref.at[columns, :], held.at[slot], sems.at[slot])


def forward_first(chain, table, x, start, w, weights, after=()):
    _, rows, depth = x.shape
    ins = [x, *(pltpu.with_memory_space_constraint(value, pltpu.HBM) for value in weights)]
    outs = [shape((4, rows, 3 * w))] * 2 + [shape((4, depth, 2 * w))] * 2
    scratch = [pltpu.VMEM((8, w, depth), BF16), pltpu.SemaphoreType.DMA((8,)), pltpu.SemaphoreType.DMA((8, 2))]

    def kernel(table_ref, in_refs, out_refs, held):
        x_ref, gate_ref, up_ref, down_ref = in_refs
        down, down_sems, sems = held

        def copies(j):
            columns = place(table_ref, (SEND + KEEP)[j], start, w)
            kept = out_refs[2 + j // 4]
            return [
                pltpu.make_async_copy(gate_ref.at[:, columns], kept.at[j % 4, :, pl.ds(0, w)], sems.at[j, 0]),
                pltpu.make_async_copy(up_ref.at[:, columns], kept.at[j % 4, :, pl.ds(w, w)], sems.at[j, 1]),
                down_copy_of(columns, down_ref, down, down_sems, j),
            ]

        for j in range(AHEAD):
            for copy in copies(j):
                copy.start()
        for j in range(8):
            for copy in copies(j):
                copy.wait()
            if j + AHEAD < 8:
                for copy in copies(j + AHEAD):
                    copy.start()
            out = out_refs[j // 4]
            both = jnp.dot(x_ref[0], out_refs[2 + j // 4][j % 4], preferred_element_type=F32)
            last = lax.dot_general(x_ref[1], down[j], CONTRACT_LAST, preferred_element_type=F32)
            out[j % 4, :, : 2 * w] = both.astype(BF16)
            out[j % 4, :, 2 * w :] = last.astype(BF16)

    return chain.call(
        kernel, "forward_first", table, ins, [VMEM] + [ANY] * 3, outs, [VMEM] * 4, scratch=scratch, after=after
    )


def forward(chain, table, kind, x, first_row, start, w, cache, down_weight, received=None, after=()):
    _, rows, depth = x.shape
    rows -= first_row
    ins = [
        x,
        cache,
        pltpu.with_memory_space_constraint(down_weight, pltpu.HBM),
    ]
    in_specs = [VMEM, VMEM, ANY]
    if kind == "keep":
        ins.append(received)
        in_specs.append(VMEM)
        outs = [shape((2, rows, 3 * w)), shape((2, rows, 3 * w))]
    else:
        outs = [shape((4, rows, 3 * w))]
    scratch = [pltpu.VMEM((4, w, depth), BF16), pltpu.SemaphoreType.DMA((4,))]

    def kernel(table_ref, in_refs, out_refs, held):
        x_ref, gate_up, down_ref = in_refs[:3]
        down, sems = held

        def put(j, columns, value):
            if kind == "keep":
                value = value + in_refs[3][j, :, columns].astype(F32)
                out_refs[j // 2][j % 2, :, columns] = value.astype(BF16)
            else:
                out_refs[0][j, :, columns] = value.astype(BF16)

        def down_copy(j):
            columns = place(table_ref, (KEEP if kind == "keep" else SEND)[j], start, w)
            return down_copy_of(columns, down_ref, down, sems, j)

        for j in range(4):
            down_copy(j).start()
        for j in range(4):
            put(j, slice(0, 2 * w), jnp.dot(x_ref[0, first_row:], gate_up[j], preferred_element_type=F32))
        for j in range(4):
            down_copy(j).wait()
            put(
                j, slice(2 * w, 3 * w),
                lax.dot_general(x_ref[1, first_row:], down[j], CONTRACT_LAST, preferred_element_type=F32),
            )

    return chain.call(
        kernel, "forward_" + kind, table, ins, in_specs, outs, [VMEM] * len(outs), scratch=scratch, after=after
    )


def add_first(chain, table, terms, received, after=()):
    _, rows, lanes = terms.shape

    def kernel(table_ref, ins, outs, _):
        for j in range(4):
            outs[j // 2][j % 2] = (ins[0][j].astype(F32) + ins[1][j].astype(F32)).astype(BF16)

    return chain.call(
        kernel, "add_first", table, [terms, received], [VMEM] * 2, [shape((2, rows, lanes))] * 2, [VMEM] * 2,
        after=after, spare=4,
    )


def add_later(chain, table, kept, received, after=()):
    _, rows, lanes = kept.shape

    def kernel(table_ref, ins, outs, _):
        outs[0][...] = (ins[0][0].astype(F32) + ins[1][1].astype(F32)).astype(BF16)

    (out,) = chain.call(
        kernel, "add_later", table, [kept, received], [VMEM] * 2, [shape((rows, lanes))], [VMEM], after=after, spare=4
    )
    return out


def deltas(chain, table, own, rest, planes, after=()):
    _, own_rows, lanes = own[0].shape
    w = lanes // 3
    blocks = rest[0].shape[1] // own_rows
    rows = own_rows * (blocks + 1)

    def kernel(table_ref, ins, outs, _):
        for block in range(blocks + 1):
            keep, second, third = ins[3:] if block else ins[:3]
            source = pl.ds(max(block - 1, 0) * own_rows, own_rows)
            summed = [
                keep[1, source, i * w : (i + 1) * w].astype(F32)
                + second[0, source, i * w : (i + 1) * w].astype(F32)
                + third[source, i * w : (i + 1) * w].astype(F32)
                for i in range(3)
            ]
            hidden, gate_delta, up_delta = swiglu_back(*summed)
            values = (gate_delta, up_delta, hidden)
            for i, plane in enumerate(planes):
                outs[0][block * own_rows : (block + 1) * own_rows, i * w : (i + 1) * w] = values[plane]

    (result,) = chain.call(
        kernel, "deltas", table, [*own, *rest], [VMEM] * 6, [shape((rows, len(planes) * w))], [VMEM], after=after, spare=4
    )
    return result


CACHE_SLOT = (3, 2, 0, 1)


def backward(
    chain, table, pieces, entries, planes, start, caches, x, factor, total, gate_up_grads, down_grad, width, parts, blocks=0,
    stack=False, after=(),
):
    rows, lanes = pieces[0].shape[-2:]
    w = lanes // planes
    slots = []
    for i, piece in enumerate(pieces):
        slots += [(i, None)] if piece.ndim == 2 else [(i, s) for s in range(piece.shape[0])]
    count = len(slots)
    do_input, do_weights, do_down = ("input" in parts), ("weights" in parts), ("down" in parts)
    depth = x.shape[2]
    ins, in_specs, outs, out_specs, scratch, aliases = list(pieces), [VMEM] * len(pieces), [], [], [], {}
    names_in, names_out, names = {}, {}, {}

    def add_in(name, array, spec=VMEM):
        names_in[name] = len(ins)
        ins.append(array)
        in_specs.append(spec)

    def add_scratch(name, kind):
        names[name] = len(scratch)
        scratch.append(kind)

    def add_out(name, dims, kind=BF16, spec=VMEM, alias=None):
        names_out[name] = len(outs)
        if alias is not None:
            aliases[len(ins)] = len(outs)
            add_in("alias_" + name, pltpu.with_memory_space_constraint(alias, pltpu.HBM), spec)
        outs.append(shape(dims, kind))
        out_specs.append(spec)

    if do_weights or do_down:
        add_in("x", x)
    if stack:
        add_out("stack", (count, rows, lanes))
    if do_input:
        for i, cache in enumerate(caches):
            add_in(f"weights{i}", cache)
        if total is not None:
            add_in("total", total)
        if blocks:
            part = rows // blocks
            for i in range(blocks):
                add_out(f"total{i}", (part, depth), BF16 if i else F32)
            add_scratch("acc", pltpu.VMEM((rows, depth), F32))
        else:
            add_out("total", (rows, depth), F32)
    if do_weights:
        for i, name in enumerate(("gate_grad", "up_grad")):
            add_out(name, (depth, width), spec=ANY, alias=gate_up_grads and gate_up_grads[i])
        add_scratch("grads", pltpu.VMEM((2, depth, 2 * w), BF16))
        add_scratch("grad_sems", pltpu.SemaphoreType.DMA((2, 2)))
    if do_down:
        add_out("down_grad", (width, depth), spec=ANY, alias=down_grad)
        add_scratch("downs", pltpu.VMEM((2, w, depth), BF16))
        add_scratch("down_sems", pltpu.SemaphoreType.DMA((2,)))

    def kernel(table_ref, in_refs, out_refs, held):
        def at(name):
            return held[names[name]]

        def given(name):
            return in_refs[names_in[name]]

        def result(name):
            return out_refs[names_out[name]]

        def piece(s, columns):
            i, inner = slots[s]
            return in_refs[i][:, columns] if inner is None else in_refs[i][inner, :, columns]

        def grad_copy(s, i):
            return pltpu.make_async_copy(
                at("grads").at[s % 2, :, pl.ds(i * w, w)],
                result(("gate_grad", "up_grad")[i]).at[:, place(table_ref, entries[s], start, w)],
                at("grad_sems").at[s % 2, i],
            )

        def down_copy(s):
            return pltpu.make_async_copy(
                at("downs").at[s % 2],
                result("down_grad").at[place(table_ref, entries[s], start, w), :],
                at("down_sems").at[s % 2],
            )

        if do_input:
            acc = at("acc") if blocks else result("total")
        for s in range(count):
            if do_weights:
                if s >= 2:
                    grad_copy(s - 2, 0).wait()
                    grad_copy(s - 2, 1).wait()
                for lower in range(0, depth, depth // 2):
                    some = slice(lower, lower + depth // 2)
                    product = lax.dot_general(
                        given("x")[0, :, some], piece(s, slice(0, 2 * w)), CONTRACT_FIRST, preferred_element_type=F32
                    )
                    at("grads")[s % 2, some] = (product * factor).astype(BF16)
                grad_copy(s, 0).start()
                grad_copy(s, 1).start()
            if do_down:
                if s >= 2:
                    down_copy(s - 2).wait()
                product = lax.dot_general(
                    piece(s, slice((planes - 1) * w, planes * w)), given("x")[1], CONTRACT_FIRST,
                    preferred_element_type=F32,
                )
                at("downs")[s % 2] = (product * factor).astype(BF16)
                down_copy(s).start()
            if do_input:
                term = lax.dot_general(
                    piece(s, slice(0, 2 * w)), given(f"weights{s // 4}")[CACHE_SLOT[s % 4]], CONTRACT_LAST,
                    preferred_element_type=F32,
                )
                if s or total is not None:
                    term = term + (acc if s else given("total"))[...]
                acc[...] = term
            if stack:
                result("stack")[s] = piece(s, slice(0, lanes))
        if do_input and blocks:
            for i in range(blocks):
                result(f"total{i}")[...] = acc[i * part : (i + 1) * part].astype(BF16 if i else F32)
        for s in range(max(count - 2, 0), count):
            if do_weights:
                grad_copy(s, 0).wait()
                grad_copy(s, 1).wait()
            if do_down:
                down_copy(s).wait()

    results = chain.call(
        kernel, "backward_" + "_".join(parts), table, ins, in_specs, outs, out_specs,
        scratch=scratch, aliases=aliases, after=after, spare=14,
    )
    return {name: results[i] for name, i in names_out.items()}


def exchange(value, masks):
    return lax.ppermute(value, "row", [(i, i ^ masks[i % 2]) for i in range(8)])


CORE, SECOND, THIRD = (1, 1), (2, 4), (4, 2)
DELTAS, HIDDEN, ALL = (0, 1), (2,), (0, 1, 2)


def chunk_widths(width):
    units = width // (8 * LANES)
    parts = [u for u in (units * 2 // 7, units - 2 * (units * 2 // 7), units * 2 // 7) if u]
    return [8 * LANES * u for u in parts]


def local(n_col, layer_input, out_grad, gate_weight, up_weight, down_weight):
    own_rows, depth = layer_input.shape
    width = gate_weight.shape[1]
    tokens = own_rows * n_col
    factor = 1.0 / tokens**0.5
    weights = (gate_weight, up_weight, down_weight)

    me = lax.axis_index("row").astype(jnp.int32)
    second = jnp.where(me % 2 == 0, SECOND[0], SECOND[1])
    third = 6 - second
    zero = jnp.zeros_like(me)
    steps = [
        second, zero + 6, third, zero,
        third + 1, zero + 7, second + 1, zero + 1,
        zero, third, second, zero + 6,
        zero + 1, second + 1, third + 1, zero + 7,
    ]
    table = me ^ jnp.stack(steps)

    own = jnp.stack([layer_input, out_grad])
    others = [
        lax.ppermute(own, "col", [(c, (c - j) % n_col) for c in range(n_col)]) for j in range(1, n_col)
    ]

    widths = chunk_widths(width)
    n = len(widths)
    w = [c // 8 for c in widths]
    start = [sum(widths[:k]) for k in range(n)]
    chain = Chain(jnp.zeros((8, LANES), F32))

    swapped, kept, sent2, got3 = {}, {}, {}, {}
    near, far, cache, terms, tokens_x = {}, {}, {}, {}, []
    state = {"total": None, "gate_up": None, "down": None}

    def first(k, after=()):
        out, terms[k], cache["send", k], cache["keep", k] = forward_first(
            chain, table, own, start[k], w[k], weights, after
        )
        swapped["own", k] = exchange(out, CORE)

    def first_sum(k, after=()):
        out, kept["own", k] = add_first(chain, table, terms[k], swapped["own", k], after)
        sent2["own", k] = exchange(out, SECOND)

    def run(kind, k, after=()):
        results = forward(
            chain, table, kind, tokens_x[0], own_rows, start[k], w[k], cache[kind, k], down_weight,
            swapped.get(("rest", k)), after,
        )
        if kind == "send":
            swapped["rest", k] = exchange(results[0], CORE)
        else:
            sent2["rest", k] = exchange(results[0], SECOND)
            kept["rest", k] = results[1]

    def add(g, k, after=()):
        out = add_later(chain, table, kept[g, k], sent2[g, k], after)
        got3[g, k] = exchange(out, THIRD)

    def sources(g, k):
        return (kept[g, k], sent2[g, k], got3[g, k])

    def make(k, planes, after=()):
        mine = deltas(chain, table, sources("own", k), sources("rest", k), planes, after)
        third_one = exchange(mine, THIRD)
        near[k, planes] = [mine, third_one, exchange(mine, SECOND), exchange(third_one, SECOND)]

    def back(k, planes, parts, which, blocks=0, stack=False, after=()):
        pieces, entries = {
            "near": (near.get((k, planes)), NEAR),
            "far": (far.get((k, planes)), FAR),
            "both": ((near.get((k, planes)) or []) + (far.get((k, planes)) or []), NEAR + FAR),
        }[which]
        used = [cache[kind, k] for kind in {"near": ["keep"], "far": ["send"], "both": ["keep", "send"]}[which]]
        out = backward(
            chain, table, pieces, entries, len(planes), start[k], used, tokens_x[0], factor, state["total"],
            state["gate_up"], state["down"], width, parts, blocks, stack, after,
        )
        if stack:
            far[k, planes] = [exchange(out["stack"], CORE)]
        if "total" in out:
            state["total"] = out["total"]
        if blocks:
            state["total"] = [out[f"total{i}"] for i in range(blocks)]
        if "gate_grad" in out:
            state["gate_up"] = (out["gate_grad"], out["up_grad"])
        if "down_grad" in out:
            state["down"] = out["down_grad"]

    every_part = ("input", "weights", "down")
    first(0)
    first(1)
    first_sum(0)
    first(2)
    first_sum(1)
    add("own", 0)
    first_sum(2)
    add("own", 1)
    tokens_x.append(gather_tokens(chain, table, [own, *others]))
    run("send", 0)
    add("own", 2, after=[got3["own", 0]])
    run("send", 1)
    run("keep", 0, after=[got3["own", 1]])
    run("keep", 1, after=[got3["own", 2]])
    run("send", 2)
    add("rest", 0)
    run("keep", 2)
    make(0, ALL)
    add("rest", 1)
    add("rest", 2, after=[near[0, ALL][1]])
    make(1, ALL)
    back(0, ALL, every_part, "near", stack=True)
    make(2, DELTAS, after=[near[1, ALL][1]])
    back(0, ALL, every_part, "far")
    back(1, ALL, every_part, "near", stack=True, after=[near[2, DELTAS][1]])
    make(2, HIDDEN)
    back(1, ALL, every_part, "far")
    back(2, DELTAS, ("input",), "near", stack=True, after=[near[2, HIDDEN][1]])
    back(2, DELTAS, ("input",), "far", blocks=n_col)
    moved = [
        lax.ppermute(state["total"][j], "col", [(c, (c + j) % n_col) for c in range(n_col)]) for j in range(1, n_col)
    ]
    back(2, DELTAS, ("weights",), "both")
    back(2, HIDDEN, ("down",), "near", stack=True)
    back(2, HIDDEN, ("down",), "far")
    input_grad = (state["total"][0] + sum(m.astype(F32) for m in moved)).astype(BF16)
    return (input_grad, *state["gate_up"], state["down"])


def solution(mesh):
    n_col = mesh.shape["col"]

    def run(layer_input, out_grad, gate_weight, up_weight, down_weight):
        fits = (
            mesh.shape["row"] == 8
            and n_col > 1
            and layer_input.shape[0] % 16 == 0
            and layer_input.shape[1] % LANES == 0
            and gate_weight.shape[1] % (8 * LANES) == 0
            and gate_weight.shape[1] >= 4 * 8 * LANES
        )
        body = functools.partial(local, n_col) if fits else plain
        return body(layer_input, out_grad, gate_weight, up_weight, down_weight)

    placed = (P("col", "row"), P("col", "row"), P("row", "col"), P("row", "col"), P("col", "row"))
    return jax.shard_map(
        run,
        mesh=mesh,
        in_specs=placed,
        out_specs=(P("col", "row"), P("row", "col"), P("row", "col"), P("col", "row")),
        check_vma=False,
    )
```

```python
import functools
import math

import jax
import jax.numpy as jnp
from jax import lax
from jax.experimental import pallas as pl
from jax.experimental.pallas import tpu as pltpu
from jax.sharding import PartitionSpec as P

BF16 = jnp.bfloat16
F32 = jnp.float32
LANES = 128
CONTRACT_LAST = (((1,), (1,)), ((), ()))
CONTRACT_FIRST = (((0,), (0,)), ((), ()))


def swiglu_back(gate, up, hidden_grad):
    sigma = jax.nn.sigmoid(gate)
    swish = gate * sigma
    hidden = (swish * up).astype(BF16)
    up_delta = (hidden_grad * swish).astype(BF16)
    gate_delta = (hidden_grad * up * sigma * (1.0 + gate * (1.0 - sigma))).astype(BF16)
    return (hidden, gate_delta, up_delta)


def plain(layer_input, out_grad, gate_weight, up_weight, down_weight):
    inputs, cots = (
        lax.all_gather(layer_input, "col", axis=0, tiled=True),
        lax.all_gather(out_grad, "col", axis=0, tiled=True),
    )
    tokens = inputs.shape[0]
    width = gate_weight.shape[1]
    both_weights = jnp.concatenate([gate_weight, up_weight], axis=1)
    gate_up = jnp.dot(inputs, both_weights, preferred_element_type=F32)
    hidden_grad = lax.dot_general(cots, down_weight, CONTRACT_LAST, preferred_element_type=F32)
    summed = lax.psum_scatter(
        jnp.concatenate([gate_up, hidden_grad], axis=1).astype(BF16),
        "row",
        scatter_dimension=0,
        tiled=True,
    ).astype(F32)
    hidden, gate_delta, up_delta = swiglu_back(
        summed[:, :width], summed[:, width : 2 * width], summed[:, 2 * width :]
    )
    hidden = lax.all_gather(hidden, "row", axis=0, tiled=True)
    gate_delta = lax.all_gather(gate_delta, "row", axis=0, tiled=True)
    up_delta = lax.all_gather(up_delta, "row", axis=0, tiled=True)
    down_sum = lax.dot_general(hidden, cots, CONTRACT_FIRST, preferred_element_type=F32)
    gate_sum = lax.dot_general(inputs, gate_delta, CONTRACT_FIRST, preferred_element_type=F32)
    up_sum = lax.dot_general(inputs, up_delta, CONTRACT_FIRST, preferred_element_type=F32)
    term = lax.dot_general(gate_delta, gate_weight, CONTRACT_LAST, preferred_element_type=F32)
    term = term + lax.dot_general(up_delta, up_weight, CONTRACT_LAST, preferred_element_type=F32)
    factor = 1.0 / tokens**0.5
    input_grad = lax.psum_scatter(term.astype(BF16), "col", scatter_dimension=0, tiled=True)
    return (
        input_grad,
        (gate_sum * factor).astype(BF16),
        (up_sum * factor).astype(BF16),
        (down_sum * factor).astype(BF16),
    )


class Chain:
    def __init__(self, token):
        self.token = token

    def call(self, kernel, name, table, ins, in_specs, outs, out_specs, scratch=(), aliases=None, after=(), spare=6):
        extra = [self.token, *after]
        n_in, n_extra, n_out = len(ins), len(extra), len(outs)

        def body(table_ref, *refs):
            in_refs = refs[:n_in]
            out_refs = refs[n_in + n_extra : n_in + n_extra + n_out]
            token_ref = refs[n_in + n_extra + n_out]
            scratch_refs = refs[n_in + n_extra + n_out + 1 :]
            token_ref[...] = jnp.zeros_like(token_ref)
            kernel(table_ref, in_refs, out_refs, scratch_refs)

        held = 0
        for kind in scratch:
            if kind.dtype in (BF16, F32):
                held += math.prod(kind.shape) * jnp.dtype(kind.dtype).itemsize
        *results, self.token = pl.pallas_call(
            body,
            name=name,
            grid_spec=pltpu.PrefetchScalarGridSpec(
                num_scalar_prefetch=1,
                grid=(),
                in_specs=[*in_specs, *[ANY] * n_extra],
                out_specs=[*out_specs, VMEM],
                scratch_shapes=list(scratch),
            ),
            out_shape=[*outs, jax.ShapeDtypeStruct((8, LANES), F32)],
            input_output_aliases={1 + i: o for i, o in (aliases or {}).items()},
            compiler_params=pltpu.CompilerParams(vmem_limit_bytes=held + spare * 2**20),
            cost_estimate=pl.CostEstimate(flops=COST, bytes_accessed=COST, transcendentals=0),
        )(table, *ins, *extra)
        return results


ANY = pl.BlockSpec(memory_space=pl.ANY)
VMEM = pl.BlockSpec(memory_space=pltpu.VMEM)
COST = 10**12


def shape(dims, kind=BF16):
    return jax.ShapeDtypeStruct(dims, kind)


KEEP, SEND, NEAR, FAR = (0, 1, 2, 3), (4, 5, 6, 7), (8, 9, 10, 11), (12, 13, 14, 15)


def place(table_ref, entry, start, w):
    return pl.ds(pl.multiple_of(start + table_ref[entry] * w, LANES), w)


def gather_tokens(chain, table, parts, after=()):
    two, own_rows, depth = parts[0].shape
    count = len(parts)

    def kernel(table_ref, ins, outs, _):
        for i in range(count):
            outs[0][:, i * own_rows : (i + 1) * own_rows] = ins[i][...]
        outs[1][...] = outs[0][0].T

    return chain.call(
        kernel, "gather_tokens", table, parts, [VMEM] * count,
        [shape((two, count * own_rows, depth)), shape((depth, count * own_rows))], [VMEM] * 2, after=after, spare=8,
    )


def down_copy_of(columns, down_ref, held, sems, slot):
    return pltpu.make_async_copy(down_ref.at[columns, :], held.at[slot], sems.at[slot])


def keep_weights(chain, table, start, w, weights, after=()):
    depth = weights[0].shape[0]
    ins = [pltpu.with_memory_space_constraint(value, pltpu.HBM) for value in weights]

    def kernel(table_ref, in_refs, out_refs, held):
        copies = []
        for j in range(8):
            columns = place(table_ref, (SEND + KEEP)[j], start, w)
            for i in range(2):
                copies.append(
                    pltpu.make_async_copy(
                        in_refs[i].at[:, columns], out_refs[j // 4].at[j % 4, :, pl.ds(i * w, w)], held[0].at[j, i]
                    )
                )
                copies[-1].start()
        for copy in copies:
            copy.wait()

    return chain.call(
        kernel, "keep_weights", table, ins, [ANY] * 2, [shape((4, depth, 2 * w))] * 2, [VMEM] * 2,
        scratch=[pltpu.SemaphoreType.DMA((8, 2))], after=after, spare=2,
    )


def forward(chain, table, x, down_weight, jobs, after=()):
    _, rows, depth = x.shape
    ins = [x, pltpu.with_memory_space_constraint(down_weight, pltpu.HBM)]
    in_specs = [VMEM, ANY]
    outs, scratch, layout = [], [], []
    for kind, start, w, cache, received in jobs:
        layout.append((kind, start, w, len(ins), len(outs), len(scratch)))
        ins.append(cache)
        if kind == "keep":
            ins.append(received)
            outs += [shape((2, rows, 3 * w)), shape((2, rows, 3 * w))]
        else:
            outs.append(shape((4, rows, 3 * w)))
        scratch += [pltpu.VMEM((4, w, depth), BF16), pltpu.SemaphoreType.DMA((4,))]

    def kernel(table_ref, in_refs, out_refs, held):
        x_ref, down_ref = in_refs[:2]

        def down_copy(job, j):
            kind, start, w, _, _, at = job
            columns = place(table_ref, (KEEP if kind == "keep" else SEND)[j], start, w)
            return down_copy_of(columns, down_ref, held[at], held[at + 1], j)

        for job in layout:
            for j in range(4):
                down_copy(job, j).start()
        for job in layout:
            kind, start, w, first_in, first_out, at = job

            def put(j, columns, value, kind=kind, first_in=first_in, first_out=first_out):
                if kind == "keep":
                    value = value + in_refs[first_in + 1][j, :, columns].astype(F32)
                    out_refs[first_out + j // 2][j % 2, :, columns] = value.astype(BF16)
                else:
                    out_refs[first_out][j, :, columns] = value.astype(BF16)

            for j in range(4):
                put(j, slice(0, 2 * w), jnp.dot(x_ref[0], in_refs[first_in][j], preferred_element_type=F32))
            for j in range(4):
                down_copy(job, j).wait()
                put(
                    j, slice(2 * w, 3 * w),
                    lax.dot_general(x_ref[1], held[at][j], CONTRACT_LAST, preferred_element_type=F32),
                )

    return chain.call(
        kernel, "forward_" + "_".join(job[0] for job in jobs), table, ins, in_specs + [VMEM] * (len(ins) - 2), outs,
        [VMEM] * len(outs), scratch=scratch, after=after, spare=4 + 4 * len(jobs),
    )


def combine(chain, table, jobs, after=()):
    ins, outs, layout = [], [], []
    for kind, *arrays in jobs:
        layout.append((kind, len(ins)))
        outs.append(shape(arrays[0].shape[1:]))
        ins += arrays

    def kernel(table_ref, in_refs, out_refs, _):
        for (kind, at), out in zip(layout, out_refs):
            rows, lanes = out.shape
            w = lanes // 3
            parts = 4 if rows % 64 == 0 else 1
            for part in range(parts):
                some = slice(part * (rows // parts), (part + 1) * (rows // parts))
                if kind == "add":
                    out[some] = (in_refs[at][0, some].astype(F32) + in_refs[at + 1][1, some].astype(F32)).astype(BF16)
                    continue
                summed = [
                    in_refs[at][1, some, i * w : (i + 1) * w].astype(F32)
                    + in_refs[at + 1][0, some, i * w : (i + 1) * w].astype(F32)
                    + in_refs[at + 2][some, i * w : (i + 1) * w].astype(F32)
                    for i in range(3)
                ]
                hidden, gate_delta, up_delta = swiglu_back(*summed)
                for i, value in enumerate((gate_delta, up_delta, hidden)):
                    out[some, i * w : (i + 1) * w] = value

    return chain.call(
        kernel, "_".join(job[0] for job in jobs), table, ins, [VMEM] * len(ins), outs, [VMEM] * len(outs), after=after,
        spare=12,
    )


CACHE_SLOT = (3, 2, 0, 1)


def backward(
    chain, table, pieces, entries, planes, start, caches, x, x_turned, factor, total, gate_up_grads, down_grad, width, parts, blocks=0,
    stack=False, only=None, after=(),
):
    rows, lanes = pieces[0].shape[-2:]
    w = lanes // planes
    slots = []
    for i, piece in enumerate(pieces):
        slots += [(i, None)] if piece.ndim == 2 else [(i, s) for s in range(piece.shape[0])]
    count = len(slots)
    order = list(range(count)) if only is None else [only]
    do_input, do_weights, do_down = ("input" in parts), ("weights" in parts), ("down" in parts)
    depth = x.shape[2]
    ins, in_specs, outs, out_specs, scratch, aliases = list(pieces), [VMEM] * len(pieces), [], [], [], {}
    names_in, names_out, names = {}, {}, {}

    def add_in(name, array, spec=VMEM):
        names_in[name] = len(ins)
        ins.append(array)
        in_specs.append(spec)

    def add_scratch(name, kind):
        names[name] = len(scratch)
        scratch.append(kind)

    def add_out(name, dims, kind=BF16, spec=VMEM, alias=None):
        names_out[name] = len(outs)
        if alias is not None:
            aliases[len(ins)] = len(outs)
            add_in("alias_" + name, pltpu.with_memory_space_constraint(alias, pltpu.HBM), spec)
        outs.append(shape(dims, kind))
        out_specs.append(spec)

    if do_weights:
        add_in("turned", x_turned)
    if do_down:
        add_in("x", x)
    if stack:
        add_out("stack", (count, rows, lanes))
    if do_input:
        for i, cache in enumerate(caches):
            add_in(f"weights{i}", cache)
        if total is not None:
            add_in("total", total)
        if blocks:
            part = rows // blocks
            for i in range(blocks):
                add_out(f"total{i}", (part, depth), BF16 if i else F32)
            add_scratch("acc", pltpu.VMEM((rows, depth), F32))
        else:
            add_out("total", (rows, depth), F32)
    if do_weights:
        for i, name in enumerate(("gate_grad", "up_grad")):
            add_out(name, (depth, width), spec=ANY, alias=gate_up_grads and gate_up_grads[i])
        add_scratch("grads", pltpu.VMEM((2, depth, 2 * w), BF16))
        add_scratch("grad_sems", pltpu.SemaphoreType.DMA((2, 2)))
    if do_down:
        add_out("down_grad", (width, depth), spec=ANY, alias=down_grad)
        add_scratch("downs", pltpu.VMEM((2, w, depth), BF16))
        add_scratch("down_sems", pltpu.SemaphoreType.DMA((2,)))

    def kernel(table_ref, in_refs, out_refs, held):
        def at(name):
            return held[names[name]]

        def given(name):
            return in_refs[names_in[name]]

        def result(name):
            return out_refs[names_out[name]]

        def piece(s, columns):
            i, inner = slots[s]
            return in_refs[i][:, columns] if inner is None else in_refs[i][inner, :, columns]

        def grad_copy(n, i):
            return pltpu.make_async_copy(
                at("grads").at[n % 2, :, pl.ds(i * w, w)],
                result(("gate_grad", "up_grad")[i]).at[:, place(table_ref, entries[order[n]], start, w)],
                at("grad_sems").at[n % 2, i],
            )

        def down_copy(n):
            return pltpu.make_async_copy(
                at("downs").at[n % 2],
                result("down_grad").at[place(table_ref, entries[order[n]], start, w), :],
                at("down_sems").at[n % 2],
            )

        if do_input:
            acc = at("acc") if blocks else result("total")
        if stack:
            for s in range(count):
                result("stack")[s] = piece(s, slice(0, lanes))
        for n, s in enumerate(order):
            if do_weights:
                if n >= 2:
                    grad_copy(n - 2, 0).wait()
                    grad_copy(n - 2, 1).wait()
                for lower in range(0, depth, depth // 2):
                    some = slice(lower, lower + depth // 2)
                    product = jnp.dot(given("turned")[some], piece(s, slice(0, 2 * w)), preferred_element_type=F32)
                    at("grads")[n % 2, some] = (product * factor).astype(BF16)
                grad_copy(n, 0).start()
                grad_copy(n, 1).start()
            if do_down:
                if n >= 2:
                    down_copy(n - 2).wait()
                product = lax.dot_general(
                    piece(s, slice((planes - 1) * w, planes * w)), given("x")[1], CONTRACT_FIRST,
                    preferred_element_type=F32,
                )
                at("downs")[n % 2] = (product * factor).astype(BF16)
                down_copy(n).start()
            if do_input:
                term = lax.dot_general(
                    piece(s, slice(0, 2 * w)), given(f"weights{s // 4}")[CACHE_SLOT[s % 4]], CONTRACT_LAST,
                    preferred_element_type=F32,
                )
                if n or total is not None:
                    term = term + (acc if n else given("total"))[...]
                acc[...] = term
        if do_input and blocks:
            for i in range(blocks):
                result(f"total{i}")[...] = acc[i * part : (i + 1) * part].astype(BF16 if i else F32)
        for n in range(max(len(order) - 2, 0), len(order)):
            if do_weights:
                grad_copy(n, 0).wait()
                grad_copy(n, 1).wait()
            if do_down:
                down_copy(n).wait()

    results = chain.call(
        kernel, "backward_" + "_".join(parts), table, ins, in_specs, outs, out_specs,
        scratch=scratch, aliases=aliases, after=after, spare=12,
    )
    return {name: results[i] for name, i in names_out.items()}


def exchange(value, masks):
    return lax.ppermute(value, "row", [(i, i ^ masks[i % 2]) for i in range(8)])


CORE, SECOND, THIRD = (1, 1), (2, 4), (4, 2)


def chunk_widths(width):
    units = width // (8 * LANES)
    last = max(1, units // 7)
    parts = [(units - last + i) // 3 for i in range(3)] + [last]
    return [8 * LANES * u for u in parts]


def local(n_col, layer_input, out_grad, gate_weight, up_weight, down_weight):
    own_rows, depth = layer_input.shape
    width = gate_weight.shape[1]
    tokens = own_rows * n_col
    factor = 1.0 / tokens**0.5
    weights = (gate_weight, up_weight, down_weight)

    me = lax.axis_index("row").astype(jnp.int32)
    second = jnp.where(me % 2 == 0, SECOND[0], SECOND[1])
    third = 6 - second
    zero = jnp.zeros_like(me)
    steps = [
        second, zero + 6, third, zero,
        third + 1, zero + 7, second + 1, zero + 1,
        zero, third, second, zero + 6,
        zero + 1, second + 1, third + 1, zero + 7,
    ]
    table = me ^ jnp.stack(steps)

    own = jnp.stack([layer_input, out_grad])
    others = [
        lax.ppermute(own, "col", [(c, (c - j) % n_col) for c in range(n_col)]) for j in range(1, n_col)
    ]

    widths = chunk_widths(width)
    n = len(widths)
    w = [c // 8 for c in widths]
    start = [sum(widths[:k]) for k in range(n)]
    chain = Chain(jnp.zeros((8, LANES), F32))

    swapped, kept, sent2, got3 = {}, {}, {}, {}
    near, far, cache = {}, {}, {}
    state = {"total": None, "gate_up": None, "down": None}

    def run(*jobs, after=()):
        listed = [
            (kind, start[k], w[k], cache[kind, k], swapped[k] if kind == "keep" else None) for kind, k in jobs
        ]
        results = forward(chain, table, x, down_weight, listed, after)
        for kind, k in jobs:
            if kind == "send":
                swapped[k] = exchange(results.pop(0), CORE)
            else:
                sent2[k] = exchange(results.pop(0), SECOND)
                kept[k] = results.pop(0)

    def sums(*jobs, after=()):
        listed = [
            ("add", kept[k], sent2[k]) if kind == "add" else ("deltas", kept[k], sent2[k], got3[k]) for kind, k in jobs
        ]
        for (kind, k), out in zip(jobs, combine(chain, table, listed, after)):
            if kind == "add":
                got3[k] = exchange(out, THIRD)
            else:
                near[k] = [out, exchange(out, THIRD), exchange(out, SECOND)]

    def relay(k):
        held, _ = lax.optimization_barrier((near[k][1], chain.token))
        near[k].append(exchange(held, SECOND))

    def back(k, parts, which, blocks=0, stack=False, only=None, after=()):
        pieces, entries, kinds = {
            "near": (near[k], NEAR, ["keep"]),
            "nearest": (near[k][:3], NEAR, ["keep"]),
            "far": (far.get(k), FAR, ["send"]),
            "both": (near[k] + far.get(k, []), NEAR + FAR, ["keep", "send"]),
        }[which]
        out = backward(
            chain, table, pieces, entries, 3, start[k], [cache[kind, k] for kind in kinds], x, x_turned, factor,
            state["total"],
            state["gate_up"], state["down"], width, parts, blocks, stack, only, after,
        )
        if stack:
            far[k] = [exchange(out["stack"], CORE)]
        if "total" in out:
            state["total"] = out["total"]
        if blocks:
            state["total"] = [out[f"total{i}"] for i in range(blocks)]
        if "gate_grad" in out:
            state["gate_up"] = (out["gate_grad"], out["up_grad"])
        if "down_grad" in out:
            state["down"] = out["down_grad"]

    every_part = ("input", "weights", "down")
    for k in range(n):
        cache["send", k], cache["keep", k] = keep_weights(chain, table, start[k], w[k], weights[:2])
    x, x_turned = gather_tokens(chain, table, [own, *others])
    run(("send", 0))
    run(("send", 1))
    run(("keep", 0))
    run(("keep", 1), ("send", 2))
    sums(("add", 0))
    run(("keep", 2), ("send", 3))
    sums(("add", 1), ("deltas", 0))
    relay(0)
    run(("keep", 3), after=near[0][1:2])
    sums(("add", 2), ("deltas", 1), after=near[0][2:3])
    relay(1)
    back(0, every_part, "near", stack=True, after=[sent2[3]])
    sums(("add", 3), ("deltas", 2), after=near[1][1:3])
    back(0, every_part, "far")
    relay(2)
    back(1, every_part, "nearest")
    sums(("deltas", 3))
    back(1, every_part, "near", stack=True, only=3, after=near[2][1:3])
    relay(3)
    back(2, every_part, "near", stack=True, after=near[3][1:3])
    back(1, every_part, "far")
    back(3, ("input",), "near", stack=True)
    back(2, ("input",), "far")
    back(3, ("input",), "far", blocks=n_col)
    moved = [
        lax.ppermute(state["total"][j], "col", [(c, (c + j) % n_col) for c in range(n_col)]) for j in range(1, n_col)
    ]
    back(2, ("weights", "down"), "far")
    back(3, ("weights", "down"), "both")
    input_grad = (state["total"][0] + sum(m.astype(F32) for m in moved)).astype(BF16)
    return (input_grad, *state["gate_up"], state["down"])


def solution(mesh):
    n_col = mesh.shape["col"]

    def run(layer_input, out_grad, gate_weight, up_weight, down_weight):
        fits = (
            mesh.shape["row"] == 8
            and n_col > 1
            and layer_input.shape[0] % 16 == 0
            and layer_input.shape[1] % (4 * LANES) == 0
            and gate_weight.shape[1] % (8 * LANES) == 0
            and gate_weight.shape[1] >= 4 * 8 * LANES
        )
        body = functools.partial(local, n_col) if fits else plain
        return body(layer_input, out_grad, gate_weight, up_weight, down_weight)

    placed = (P("col", "row"), P("col", "row"), P("row", "col"), P("row", "col"), P("col", "row"))
    return jax.shard_map(
        run,
        mesh=mesh,
        in_specs=placed,
        out_specs=(P("col", "row"), P("row", "col"), P("row", "col"), P("col", "row")),
        check_vma=False,
    )
```

```python
import functools
import math

import jax
import jax.numpy as jnp
from jax import lax
from jax.experimental import pallas as pl
from jax.experimental.pallas import tpu as pltpu
from jax.sharding import PartitionSpec as P

BF16 = jnp.bfloat16
F32 = jnp.float32
LANES = 128
CONTRACT_LAST = (((1,), (1,)), ((), ()))
CONTRACT_FIRST = (((0,), (0,)), ((), ()))


def swiglu_back(gate, up, hidden_grad):
    sigma = jax.nn.sigmoid(gate)
    swish = gate * sigma
    hidden = (swish * up).astype(BF16)
    up_delta = (hidden_grad * swish).astype(BF16)
    gate_delta = (hidden_grad * up * sigma * (1.0 + gate * (1.0 - sigma))).astype(BF16)
    return (hidden, gate_delta, up_delta)


def plain(layer_input, out_grad, gate_weight, up_weight, down_weight):
    inputs, cots = (
        lax.all_gather(layer_input, "col", axis=0, tiled=True),
        lax.all_gather(out_grad, "col", axis=0, tiled=True),
    )
    tokens = inputs.shape[0]
    width = gate_weight.shape[1]
    both_weights = jnp.concatenate([gate_weight, up_weight], axis=1)
    gate_up = jnp.dot(inputs, both_weights, preferred_element_type=F32)
    hidden_grad = lax.dot_general(cots, down_weight, CONTRACT_LAST, preferred_element_type=F32)
    summed = lax.psum_scatter(
        jnp.concatenate([gate_up, hidden_grad], axis=1).astype(BF16),
        "row",
        scatter_dimension=0,
        tiled=True,
    ).astype(F32)
    hidden, gate_delta, up_delta = swiglu_back(
        summed[:, :width], summed[:, width : 2 * width], summed[:, 2 * width :]
    )
    hidden = lax.all_gather(hidden, "row", axis=0, tiled=True)
    gate_delta = lax.all_gather(gate_delta, "row", axis=0, tiled=True)
    up_delta = lax.all_gather(up_delta, "row", axis=0, tiled=True)
    down_sum = lax.dot_general(hidden, cots, CONTRACT_FIRST, preferred_element_type=F32)
    gate_sum = lax.dot_general(inputs, gate_delta, CONTRACT_FIRST, preferred_element_type=F32)
    up_sum = lax.dot_general(inputs, up_delta, CONTRACT_FIRST, preferred_element_type=F32)
    term = lax.dot_general(gate_delta, gate_weight, CONTRACT_LAST, preferred_element_type=F32)
    term = term + lax.dot_general(up_delta, up_weight, CONTRACT_LAST, preferred_element_type=F32)
    factor = 1.0 / tokens**0.5
    input_grad = lax.psum_scatter(term.astype(BF16), "col", scatter_dimension=0, tiled=True)
    return (
        input_grad,
        (gate_sum * factor).astype(BF16),
        (up_sum * factor).astype(BF16),
        (down_sum * factor).astype(BF16),
    )


class Chain:
    def __init__(self, token):
        self.token = token

    def call(self, kernel, name, table, ins, in_specs, outs, out_specs, scratch=(), aliases=None, after=(), spare=6):
        extra = [self.token, *after]
        n_in, n_extra, n_out = len(ins), len(extra), len(outs)

        def body(table_ref, *refs):
            in_refs = refs[:n_in]
            out_refs = refs[n_in + n_extra : n_in + n_extra + n_out]
            token_ref = refs[n_in + n_extra + n_out]
            scratch_refs = refs[n_in + n_extra + n_out + 1 :]
            token_ref[...] = jnp.zeros_like(token_ref)
            kernel(table_ref, in_refs, out_refs, scratch_refs)

        held = 0
        for kind in scratch:
            if kind.dtype in (BF16, F32):
                held += math.prod(kind.shape) * jnp.dtype(kind.dtype).itemsize
        *results, self.token = pl.pallas_call(
            body,
            name=name,
            grid_spec=pltpu.PrefetchScalarGridSpec(
                num_scalar_prefetch=1,
                grid=(),
                in_specs=[*in_specs, *[ANY] * n_extra],
                out_specs=[*out_specs, VMEM],
                scratch_shapes=list(scratch),
            ),
            out_shape=[*outs, jax.ShapeDtypeStruct((8, LANES), F32)],
            input_output_aliases={1 + i: o for i, o in (aliases or {}).items()},
            compiler_params=pltpu.CompilerParams(vmem_limit_bytes=held + spare * 2**20),
            cost_estimate=pl.CostEstimate(flops=COST, bytes_accessed=COST, transcendentals=0),
        )(table, *ins, *extra)
        return results


ANY = pl.BlockSpec(memory_space=pl.ANY)
VMEM = pl.BlockSpec(memory_space=pltpu.VMEM)
COST = 10**12


def shape(dims, kind=BF16):
    return jax.ShapeDtypeStruct(dims, kind)


KEEP, SEND, NEAR, FAR = (0, 1, 2, 3), (4, 5, 6, 7), (8, 9, 10, 11), (12, 13, 14, 15)


def place(table_ref, entry, start, w):
    return pl.ds(pl.multiple_of(start + table_ref[entry] * w, LANES), w)


def gather_tokens(chain, table, parts, after=()):
    two, own_rows, depth = parts[0].shape
    count = len(parts)

    def kernel(table_ref, ins, outs, _):
        for i in range(count):
            outs[0][:, i * own_rows : (i + 1) * own_rows] = ins[i][...]
        outs[1][...] = outs[0][0].T

    return chain.call(
        kernel, "gather_tokens", table, parts, [VMEM] * count,
        [shape((two, count * own_rows, depth)), shape((depth, count * own_rows))], [VMEM] * 2, after=after, spare=8,
    )


def down_copy_of(columns, down_ref, held, sems, slot):
    return pltpu.make_async_copy(down_ref.at[columns, :], held.at[slot], sems.at[slot])


def keep_weights(chain, table, start, w, weights, after=()):
    depth = weights[0].shape[0]
    ins = [pltpu.with_memory_space_constraint(value, pltpu.HBM) for value in weights]

    def kernel(table_ref, in_refs, out_refs, held):
        copies = []
        for j in range(8):
            columns = place(table_ref, (SEND + KEEP)[j], start, w)
            for i in range(2):
                copies.append(
                    pltpu.make_async_copy(
                        in_refs[i].at[:, columns], out_refs[j // 4].at[j % 4, :, pl.ds(i * w, w)], held[0].at[j, i]
                    )
                )
                copies[-1].start()
        for copy in copies:
            copy.wait()

    return chain.call(
        kernel, "keep_weights", table, ins, [ANY] * 2, [shape((4, depth, 2 * w))] * 2, [VMEM] * 2,
        scratch=[pltpu.SemaphoreType.DMA((8, 2))], after=after, spare=2,
    )


def forward(chain, table, x, down_weight, jobs, after=()):
    _, rows, depth = x.shape
    ins = [x, pltpu.with_memory_space_constraint(down_weight, pltpu.HBM)]
    in_specs = [VMEM, ANY]
    outs, scratch, layout = [], [], []
    for kind, start, w, cache, received in jobs:
        layout.append((kind, start, w, len(ins), len(outs), len(scratch)))
        ins.append(cache)
        if kind == "keep":
            ins.append(received)
            outs += [shape((2, rows, 3 * w)), shape((2, rows, 3 * w))]
        else:
            outs.append(shape((4, rows, 3 * w)))
        scratch += [pltpu.VMEM((4, w, depth), BF16), pltpu.SemaphoreType.DMA((4,))]

    def kernel(table_ref, in_refs, out_refs, held):
        x_ref, down_ref = in_refs[:2]

        def down_copy(job, j):
            kind, start, w, _, _, at = job
            columns = place(table_ref, (KEEP if kind == "keep" else SEND)[j], start, w)
            return down_copy_of(columns, down_ref, held[at], held[at + 1], j)

        for job in layout:
            for j in range(4):
                down_copy(job, j).start()
        for job in layout:
            kind, start, w, first_in, first_out, at = job

            def put(j, columns, value, kind=kind, first_in=first_in, first_out=first_out):
                if kind == "keep":
                    value = value + in_refs[first_in + 1][j, :, columns].astype(F32)
                    out_refs[first_out + j // 2][j % 2, :, columns] = value.astype(BF16)
                else:
                    out_refs[first_out][j, :, columns] = value.astype(BF16)

            for j in range(4):
                put(j, slice(0, 2 * w), jnp.dot(x_ref[0], in_refs[first_in][j], preferred_element_type=F32))
            for j in range(4):
                down_copy(job, j).wait()
                put(
                    j, slice(2 * w, 3 * w),
                    lax.dot_general(x_ref[1], held[at][j], CONTRACT_LAST, preferred_element_type=F32),
                )

    return chain.call(
        kernel, "forward_" + "_".join(job[0] for job in jobs), table, ins, in_specs + [VMEM] * (len(ins) - 2), outs,
        [VMEM] * len(outs), scratch=scratch, after=after, spare=4 + 4 * len(jobs),
    )


def combine(chain, table, jobs, after=()):
    ins, outs, layout = [], [], []
    for kind, *arrays in jobs:
        layout.append((kind, len(ins)))
        outs.append(shape(arrays[0].shape[1:]))
        ins += arrays

    def kernel(table_ref, in_refs, out_refs, _):
        for (kind, at), out in zip(layout, out_refs):
            rows, lanes = out.shape
            w = lanes // 3
            parts = 4 if rows % 64 == 0 else 1
            for part in range(parts):
                some = slice(part * (rows // parts), (part + 1) * (rows // parts))
                if kind == "add":
                    out[some] = (in_refs[at][0, some].astype(F32) + in_refs[at + 1][1, some].astype(F32)).astype(BF16)
                    continue
                summed = [
                    in_refs[at][1, some, i * w : (i + 1) * w].astype(F32)
                    + in_refs[at + 1][0, some, i * w : (i + 1) * w].astype(F32)
                    + in_refs[at + 2][some, i * w : (i + 1) * w].astype(F32)
                    for i in range(3)
                ]
                hidden, gate_delta, up_delta = swiglu_back(*summed)
                for i, value in enumerate((gate_delta, up_delta, hidden)):
                    out[some, i * w : (i + 1) * w] = value

    return chain.call(
        kernel, "_".join(job[0] for job in jobs), table, ins, [VMEM] * len(ins), outs, [VMEM] * len(outs), after=after,
        spare=12,
    )


CACHE_SLOT = (3, 2, 0, 1)


def backward(
    chain, table, pieces, entries, planes, start, caches, x, x_turned, factor, total, gate_up_grads, down_grad, width, parts, blocks=0,
    stack=False, only=None, after=(),
):
    rows, lanes = pieces[0].shape[-2:]
    w = lanes // planes
    slots = []
    for i, piece in enumerate(pieces):
        slots += [(i, None)] if piece.ndim == 2 else [(i, s) for s in range(piece.shape[0])]
    count = len(slots)
    order = list(range(count)) if only is None else [only]
    do_input, do_weights, do_down = ("input" in parts), ("weights" in parts), ("down" in parts)
    depth = x.shape[2]
    ins, in_specs, outs, out_specs, scratch, aliases = list(pieces), [VMEM] * len(pieces), [], [], [], {}
    names_in, names_out, names = {}, {}, {}

    def add_in(name, array, spec=VMEM):
        names_in[name] = len(ins)
        ins.append(array)
        in_specs.append(spec)

    def add_scratch(name, kind):
        names[name] = len(scratch)
        scratch.append(kind)

    def add_out(name, dims, kind=BF16, spec=VMEM, alias=None):
        names_out[name] = len(outs)
        if alias is not None:
            aliases[len(ins)] = len(outs)
            add_in("alias_" + name, pltpu.with_memory_space_constraint(alias, pltpu.HBM), spec)
        outs.append(shape(dims, kind))
        out_specs.append(spec)

    if do_weights:
        add_in("turned", x_turned)
    if do_down:
        add_in("x", x)
    if stack:
        add_out("stack", (count, rows, lanes))
    if do_input:
        for i, cache in enumerate(caches):
            add_in(f"weights{i}", cache)
        if total is not None:
            add_in("total", total)
        if blocks:
            part = rows // blocks
            for i in range(blocks):
                add_out(f"total{i}", (part, depth), BF16 if i else F32)
            add_scratch("acc", pltpu.VMEM((rows, depth), F32))
        else:
            add_out("total", (rows, depth), F32)
    if do_weights:
        for i, name in enumerate(("gate_grad", "up_grad")):
            add_out(name, (depth, width), spec=ANY, alias=gate_up_grads and gate_up_grads[i])
        add_scratch("grads", pltpu.VMEM((2, depth, 2 * w), BF16))
        add_scratch("grad_sems", pltpu.SemaphoreType.DMA((2, 2)))
    if do_down:
        add_out("down_grad", (width, depth), spec=ANY, alias=down_grad)
        add_scratch("downs", pltpu.VMEM((2, w, depth), BF16))
        add_scratch("down_sems", pltpu.SemaphoreType.DMA((2,)))

    def kernel(table_ref, in_refs, out_refs, held):
        def at(name):
            return held[names[name]]

        def given(name):
            return in_refs[names_in[name]]

        def result(name):
            return out_refs[names_out[name]]

        def piece(s, columns):
            i, inner = slots[s]
            return in_refs[i][:, columns] if inner is None else in_refs[i][inner, :, columns]

        def grad_copy(n, i):
            return pltpu.make_async_copy(
                at("grads").at[n % 2, :, pl.ds(i * w, w)],
                result(("gate_grad", "up_grad")[i]).at[:, place(table_ref, entries[order[n]], start, w)],
                at("grad_sems").at[n % 2, i],
            )

        def down_copy(n):
            return pltpu.make_async_copy(
                at("downs").at[n % 2],
                result("down_grad").at[place(table_ref, entries[order[n]], start, w), :],
                at("down_sems").at[n % 2],
            )

        if do_input:
            acc = at("acc") if blocks else result("total")
        if stack:
            for s in range(count):
                result("stack")[s] = piece(s, slice(0, lanes))
        for n, s in enumerate(order):
            if do_weights:
                if n >= 2:
                    grad_copy(n - 2, 0).wait()
                    grad_copy(n - 2, 1).wait()
                for lower in range(0, depth, depth // 2):
                    some = slice(lower, lower + depth // 2)
                    product = jnp.dot(given("turned")[some], piece(s, slice(0, 2 * w)), preferred_element_type=F32)
                    at("grads")[n % 2, some] = (product * factor).astype(BF16)
                grad_copy(n, 0).start()
                grad_copy(n, 1).start()
            if do_down:
                if n >= 2:
                    down_copy(n - 2).wait()
                product = lax.dot_general(
                    piece(s, slice((planes - 1) * w, planes * w)), given("x")[1], CONTRACT_FIRST,
                    preferred_element_type=F32,
                )
                at("downs")[n % 2] = (product * factor).astype(BF16)
                down_copy(n).start()
            if do_input:
                term = lax.dot_general(
                    piece(s, slice(0, 2 * w)), given(f"weights{s // 4}")[CACHE_SLOT[s % 4]], CONTRACT_LAST,
                    preferred_element_type=F32,
                )
                if n or total is not None:
                    term = term + (acc if n else given("total"))[...]
                acc[...] = term
        if do_input and blocks:
            for i in range(blocks):
                result(f"total{i}")[...] = acc[i * part : (i + 1) * part].astype(BF16 if i else F32)
        for n in range(max(len(order) - 2, 0), len(order)):
            if do_weights:
                grad_copy(n, 0).wait()
                grad_copy(n, 1).wait()
            if do_down:
                down_copy(n).wait()

    results = chain.call(
        kernel, "backward_" + "_".join(parts), table, ins, in_specs, outs, out_specs,
        scratch=scratch, aliases=aliases, after=after, spare=12,
    )
    return {name: results[i] for name, i in names_out.items()}


def exchange(value, masks):
    return lax.ppermute(value, "row", [(i, i ^ masks[i % 2]) for i in range(8)])


CORE, SECOND, THIRD = (1, 1), (2, 4), (4, 2)


def chunk_widths(width):
    units = width // (8 * LANES)
    last = max(1, units // 7)
    parts = [(units - last + i) // 3 for i in range(3)] + [last]
    return [8 * LANES * u for u in parts]


def local(n_col, layer_input, out_grad, gate_weight, up_weight, down_weight):
    own_rows, depth = layer_input.shape
    width = gate_weight.shape[1]
    tokens = own_rows * n_col
    factor = 1.0 / tokens**0.5
    weights = (gate_weight, up_weight, down_weight)

    me = lax.axis_index("row").astype(jnp.int32)
    second = jnp.where(me % 2 == 0, SECOND[0], SECOND[1])
    third = 6 - second
    zero = jnp.zeros_like(me)
    steps = [
        second, zero + 6, third, zero,
        third + 1, zero + 7, second + 1, zero + 1,
        zero, third, second, zero + 6,
        zero + 1, second + 1, third + 1, zero + 7,
    ]
    table = me ^ jnp.stack(steps)

    own = jnp.stack([layer_input, out_grad])
    others = [
        lax.ppermute(own, "col", [(c, (c - j) % n_col) for c in range(n_col)]) for j in range(1, n_col)
    ]

    widths = chunk_widths(width)
    n = len(widths)
    w = [c // 8 for c in widths]
    start = [sum(widths[:k]) for k in range(n)]
    chain = Chain(jnp.zeros((8, LANES), F32))

    swapped, kept, sent2, got3 = {}, {}, {}, {}
    near, far, cache = {}, {}, {}
    state = {"total": None, "gate_up": None, "down": None}

    def run(*jobs, after=()):
        listed = [
            (kind, start[k], w[k], cache[kind, k], swapped[k] if kind == "keep" else None) for kind, k in jobs
        ]
        results = forward(chain, table, x, down_weight, listed, after)
        for kind, k in jobs:
            if kind == "send":
                swapped[k] = exchange(results.pop(0), CORE)
            else:
                sent2[k] = exchange(results.pop(0), SECOND)
                kept[k] = results.pop(0)

    def sums(*jobs, after=()):
        listed = [
            ("add", kept[k], sent2[k]) if kind == "add" else ("deltas", kept[k], sent2[k], got3[k]) for kind, k in jobs
        ]
        for (kind, k), out in zip(jobs, combine(chain, table, listed, after)):
            if kind == "add":
                got3[k] = exchange(out, THIRD)
            else:
                near[k] = [out, exchange(out, THIRD), exchange(out, SECOND)]

    def relay(k):
        held, _ = lax.optimization_barrier((near[k][1], chain.token))
        near[k].append(exchange(held, SECOND))

    def back(k, parts, which, blocks=0, stack=False, only=None, after=()):
        pieces, entries, kinds = {
            "near": (near[k], NEAR, ["keep"]),
            "nearest": (near[k][:3], NEAR, ["keep"]),
            "far": (far.get(k), FAR, ["send"]),
            "both": (near[k] + far.get(k, []), NEAR + FAR, ["keep", "send"]),
        }[which]
        out = backward(
            chain, table, pieces, entries, 3, start[k], [cache[kind, k] for kind in kinds], x, x_turned, factor,
            state["total"],
            state["gate_up"], state["down"], width, parts, blocks, stack, only, after,
        )
        if stack:
            far[k] = [exchange(out["stack"], CORE)]
        if "total" in out:
            state["total"] = out["total"]
        if blocks:
            state["total"] = [out[f"total{i}"] for i in range(blocks)]
        if "gate_grad" in out:
            state["gate_up"] = (out["gate_grad"], out["up_grad"])
        if "down_grad" in out:
            state["down"] = out["down_grad"]

    every_part = ("input", "weights", "down")
    for k in range(n):
        cache["send", k], cache["keep", k] = keep_weights(chain, table, start[k], w[k], weights[:2])
    x, x_turned = gather_tokens(chain, table, [own, *others])
    run(("send", 0))
    run(("send", 1))
    run(("keep", 0))
    run(("keep", 1), ("send", 2), ("send", 3))
    sums(("add", 0))
    run(("keep", 2), ("keep", 3))
    sums(("add", 1), ("deltas", 0))
    relay(0)
    sums(("add", 2), ("deltas", 1), after=[*near[0][1:3], sent2[3]])
    relay(1)
    back(0, every_part, "near", stack=True)
    sums(("add", 3), ("deltas", 2), after=near[1][1:3])
    back(0, every_part, "far", after=near[1][3:4])
    relay(2)
    back(1, every_part, "near", stack=True)
    sums(("deltas", 3), after=near[2][1:3])
    back(2, every_part, "near", stack=True)
    relay(3)
    back(1, every_part, "far", after=near[3][1:3])
    back(3, ("input",), "near", stack=True)
    back(2, ("input",), "far")
    back(3, ("input",), "far", blocks=n_col)
    moved = [
        lax.ppermute(state["total"][j], "col", [(c, (c + j) % n_col) for c in range(n_col)]) for j in range(1, n_col)
    ]
    back(2, ("weights", "down"), "far")
    back(3, ("weights", "down"), "both")
    input_grad = (state["total"][0] + sum(m.astype(F32) for m in moved)).astype(BF16)
    return (input_grad, *state["gate_up"], state["down"])


def solution(mesh):
    n_col = mesh.shape["col"]

    def run(layer_input, out_grad, gate_weight, up_weight, down_weight):
        fits = (
            mesh.shape["row"] == 8
            and n_col > 1
            and layer_input.shape[0] % 16 == 0
            and layer_input.shape[1] % (4 * LANES) == 0
            and gate_weight.shape[1] % (8 * LANES) == 0
            and gate_weight.shape[1] >= 4 * 8 * LANES
        )
        body = functools.partial(local, n_col) if fits else plain
        return body(layer_input, out_grad, gate_weight, up_weight, down_weight)

    placed = (P("col", "row"), P("col", "row"), P("row", "col"), P("row", "col"), P("col", "row"))
    return jax.shard_map(
        run,
        mesh=mesh,
        in_specs=placed,
        out_specs=(P("col", "row"), P("row", "col"), P("row", "col"), P("col", "row")),
        check_vma=False,
    )
```
